256 devices in a mesh: occ: 8 (over x, core), vir: 32 (over z, y).
Axes of the slice: x: 4, y: 4, z: 8, core: 2. Of those that a mesh axis runs over, the one named last changes fastest.
Arguments:
- t2_tiles: bfloat16 [72, 96, 32, 4608], P(None, 'occ', 'vir'), may hold values from -6 to 6
- w_cycle: bfloat16 [96, 4, 384, 384], P('occ', None, 'vir'), may hold values from -0.03125 to 0.03125
- screen: int32 [8, 3], replicated, may hold values from 0 to 1, as said below
Outputs:
- cycle_term: bfloat16 [72, 4, 32, 4608], P('occ', None, 'vir')
The draws below stay inside these ranges and needn't reach their ends.
Inputs may be any that keep to these rules, and one draw needn't show every extreme that they name: Each row of screen keeps between 1 and 2 of the 3 virtual tiles; some row keeps exactly 2.
All inputs are finite; a program needn't handle non-finite values.
Results may differ from the reference program's by a relative error of at most 0.0012.
Values may be sent and summed in bfloat16 or wider, within the bound.
No kernel may reach another device: no remote copies, remote signals or barrier semaphores. Data moves between devices by JAX's collectives and lax.ppermute only.
A program may use at most 128 MiB of HBM per device.

```python
import jax
import jax.numpy as jnp
from jax import lax

O = 96
V = 384
BO = 12
BV = 128
MAXC = 2
COLS_J = 4
ROWS_I = 72
VBLK = 12
NBLK = 32
NOT = 8
NVT = 3


def draw_screen(key, part):
    key = jax.random.fold_in(key, 7)
    key_count, key_full, key_order = jax.random.split(key, 3)
    counts = jax.random.randint(key_count, (NOT,), 1, MAXC + 1)
    full_row = jax.random.randint(key_full, (), 0, NOT)
    counts = jnp.where(jnp.arange(NOT) == full_row, MAXC, counts)
    orders = jax.vmap(lambda single: jax.random.permutation(single, NVT))(jax.random.split(key_order, NOT))
    return (orders < counts[:, None]).astype(jnp.int32)


def levels(key, shape, cuts, least, largest):
    gain = 1.0
    for axis_at, blocks in cuts:
        heights = jax.random.uniform(jax.random.fold_in(jax.random.fold_in(key, 6), axis_at), (blocks,), jnp.float32, least / len(cuts), largest / len(cuts))
        gain = gain * jnp.repeat(jnp.exp(heights), shape[axis_at] // blocks).reshape((-1,) + (1,) * (len(shape) - 1 - axis_at))
    return gain


def bell_draw(rng, extent, scale, reach, pieces=(), dtype=jnp.bfloat16):
    entries = jax.random.normal(rng, extent, jnp.float32) * scale
    if len(pieces) > 0:
        entries = levels(rng, extent, pieces, -0.22, 0.18) * entries
    return jnp.clip(entries, min=-reach, max=reach).astype(dtype)


def setup_inputs(seed: int = 0) -> dict:
    splits = jax.random.split(jax.random.key(seed), 4)
    return {
        "t2_tiles": bell_draw(splits[0], (ROWS_I, O, NBLK, V * VBLK), 1.0, 6.0, ((1, 8), (2, 32))),
        "w_cycle": bell_draw(splits[1], (O, COLS_J, V, V), (O * V) ** -0.5, 0.03125, ((0, 8), (2, 32))),
        "screen": draw_screen(jax.random.fold_in(splits[3], 71), 0),
    }


def reference(t2_tiles, w_cycle, screen):
    keep = jnp.repeat(jnp.repeat(screen, BO, axis=0), BV, axis=1).astype(jnp.float32)
    w_natural = w_cycle.reshape(O, COLS_J, NBLK, VBLK, NBLK, VBLK)
    w_natural = jnp.transpose(w_natural, (0, 1, 3, 2, 5, 4)).reshape(O, COLS_J, V, V)
    w_full = w_natural.astype(jnp.float32) * keep[:, None, None, :]
    amp_blocks = t2_tiles.reshape(ROWS_I, O, NBLK, V, VBLK)

    def one_row(row_block):
        amp_matrix = jnp.transpose(row_block, (0, 2, 3, 1)).reshape(O, V, V).astype(jnp.float32)
        return jnp.einsum("kac,kjbc->jab", amp_matrix, w_full, precision=lax.Precision.HIGHEST)

    cycle = lax.map(one_row, amp_blocks)
    stored = cycle.reshape(ROWS_I, COLS_J, V, VBLK, NBLK)
    stored = jnp.transpose(stored, (0, 1, 4, 2, 3)).reshape(ROWS_I, COLS_J, NBLK, V * VBLK)
    return stored.astype(jnp.bfloat16)
```

```python
import jax
import jax.numpy as jnp
from jax import lax
from jax.experimental import pallas as pl
from jax.experimental.pallas import tpu as pltpu
from jax.sharding import Mesh, PartitionSpec as P

BF16 = jnp.bfloat16
F32 = jnp.float32
MIB = 1024 * 1024
BO = 12
VB = 12
Q = 32
ZN = 8
YN = 4
ON = 8
KEPT = 8
NI = 72
IL = 9
NJ = 4
LANES = 128
THIRDS = 3
UNITS = 7
WIDE = UNITS * LANES
RJ = VB * NJ
KSRC = BO * KEPT
KW = YN * KSRC


def amplitude_kernel(chosen_ref, x_ref, out_ref, pick_ref, rows_ref):
    third = pl.program_id(0)

    @pl.when(third == 0)
    def _():
        row = lax.broadcasted_iota(jnp.int32, (LANES * VB, LANES), 0)
        col = lax.broadcasted_iota(jnp.int32, (LANES * VB, LANES), 1)
        offset = row - col * VB
        for s in range(KEPT):
            pick_ref[:, s * LANES:(s + 1) * LANES] = jnp.where(
                offset == chosen_ref[s], 1.0, 0.0
            ).astype(BF16)
        for o in range(ON):
            out_ref[o * YN + YN - 1, :, (UNITS - 1) * LANES:] = jnp.zeros((KSRC, LANES), BF16)

    for pair in range(KEPT // 2):
        picked = jnp.dot(
            x_ref[...],
            pick_ref[:, pair * 2 * LANES:(pair + 1) * 2 * LANES],
            preferred_element_type=F32,
        )
        for half in range(2):
            rows_ref[pl.ds(2 * pair + half, BO * NI, stride=KEPT), :] = picked[
                :, half * LANES:(half + 1) * LANES
            ]

    def place(kp, carry):
        for i in range(NI):
            unit = third * IL + i % IL
            low = pl.multiple_of((2 * kp * NI + i) * KEPT, KEPT)
            high = pl.multiple_of(((2 * kp + 1) * NI + i) * KEPT, KEPT)
            tile = jnp.concatenate(
                [rows_ref[pl.ds(low, KEPT), :], rows_ref[pl.ds(high, KEPT), :]], axis=0
            ).astype(BF16)
            out_ref[
                (i // IL) * YN + unit // UNITS,
                pl.ds(pl.multiple_of(kp * 2 * KEPT, 2 * KEPT), 2 * KEPT),
                pl.ds(pl.multiple_of((unit % UNITS) * LANES, LANES), LANES),
            ] = tile
        return carry

    lax.fori_loop(0, BO // 2, place, 0)


def relay_amplitudes(chosen, x):
    return pl.pallas_call(
        amplitude_kernel,
        grid=(THIRDS,),
        in_specs=[
            pl.BlockSpec(memory_space=pltpu.SMEM),
            pl.BlockSpec((BO * NI, LANES * VB), lambda t: (0, t)),
        ],
        out_specs=pl.BlockSpec((ON * YN, KSRC, WIDE), lambda t: (0, 0, 0)),
        out_shape=jax.ShapeDtypeStruct((ON * YN, KSRC, WIDE), BF16),
        scratch_shapes=[
            pltpu.VMEM((LANES * VB, KEPT * LANES), BF16),
            pltpu.VMEM((BO * NI * KEPT, LANES), F32),
        ],
        compiler_params=pltpu.CompilerParams(vmem_limit_bytes=48 * MIB),
        cost_estimate=pl.CostEstimate(
            flops=2 * BO * NI * THIRDS * LANES * VB * KEPT * LANES,
            bytes_accessed=14 * MIB,
            transcendentals=0,
        ),
        name="relay_amplitudes",
    )(chosen, x)


def integral_kernel(chosen_ref, w_ref, out_ref, pick_ref, sum_ref):
    row = lax.broadcasted_iota(jnp.int32, (Q * VB, KW), 0)
    col = lax.broadcasted_iota(jnp.int32, (Q * VB, KW), 1)
    y_of = col // KSRC
    inner = col - y_of * KSRC
    wanted = jnp.full((Q * VB, KW), -1, jnp.int32)
    for s in range(KEPT):
        wanted = jnp.where((inner == s) & (chosen_ref[s] >= 0), y_of * VB + chosen_ref[s], wanted)
    for z in range(ZN):
        pick_ref[:, z * KW:(z + 1) * KW] = jnp.where(
            (wanted >= 0) & (row - z * YN * VB == wanted), 1.0, 0.0
        ).astype(BF16)
    sum_ref[...] = jnp.zeros_like(sum_ref)
    for k in range(BO):
        w = w_ref[k * RJ:(k + 1) * RJ, :]
        for z in range(ZN):
            part = jnp.dot(w, pick_ref[:, z * KW:(z + 1) * KW], preferred_element_type=F32)
            sum_ref[z * RJ:(z + 1) * RJ, :] += pltpu.roll(part, k * KEPT, 1) if k else part
    out_ref[...] = sum_ref[...].astype(BF16)


def relay_integrals(chosen, w):
    return pl.pallas_call(
        integral_kernel,
        in_specs=[
            pl.BlockSpec(memory_space=pltpu.SMEM),
            pl.BlockSpec(memory_space=pltpu.VMEM),
        ],
        out_specs=pl.BlockSpec(memory_space=pltpu.VMEM),
        out_shape=jax.ShapeDtypeStruct((ZN * RJ, KW), BF16),
        scratch_shapes=[
            pltpu.VMEM((Q * VB, ZN * KW), BF16),
            pltpu.VMEM((ZN * RJ, KW), F32),
        ],
        compiler_params=pltpu.CompilerParams(vmem_limit_bytes=32 * MIB),
        cost_estimate=pl.CostEstimate(
            flops=2 * BO * RJ * Q * VB * ZN * KW, bytes_accessed=MIB, transcendentals=0
        ),
        name="relay_integrals",
    )(chosen, w)


def contract_kernel(w_ref, a_ref, out_ref):
    left = jnp.concatenate([w_ref[o, 0] for o in range(ON)], axis=1)
    product = jnp.dot(left, a_ref[...], preferred_element_type=F32)
    out_ref[...] = product.reshape(ZN, RJ, WIDE)


def contract(w, a):
    return pl.pallas_call(
        contract_kernel,
        grid=(YN,),
        in_specs=[
            pl.BlockSpec((ON, 1, ZN * RJ, KW), lambda y: (0, y, 0, 0)),
            pl.BlockSpec((ON * KW, WIDE), lambda y: (0, 0)),
        ],
        out_specs=pl.BlockSpec((ZN, RJ, WIDE), lambda y: (0, y, 0)),
        out_shape=jax.ShapeDtypeStruct((ZN, YN * RJ, WIDE), F32),
        compiler_params=pltpu.CompilerParams(vmem_limit_bytes=48 * MIB),
        cost_estimate=pl.CostEstimate(
            flops=2 * YN * ZN * RJ * ON * KW * WIDE, bytes_accessed=20 * MIB, transcendentals=0
        ),
        name="contract",
    )(w, a)


def store_kernel(d_ref, out_ref):
    row = lax.broadcasted_iota(jnp.int32, (LANES, LANES * VB), 0)
    col = lax.broadcasted_iota(jnp.int32, (LANES, LANES * VB), 1)
    spread = jnp.where(col // VB == row, 1.0, 0.0).astype(BF16)
    place = lax.broadcasted_iota(jnp.int32, (RJ, LANES * VB), 0) // NJ
    minor = lax.broadcasted_iota(jnp.int32, (RJ, LANES * VB), 1) % VB
    own = place == minor
    for il in range(IL):
        for third in range(THIRDS):
            unit = third * IL + il
            y, slot = unit // UNITS, unit % UNITS
            piece = d_ref[y, :, slot * LANES:(slot + 1) * LANES]
            wide = jnp.dot(piece, spread, preferred_element_type=F32)
            wide = jnp.where(own, wide, 0.0)
            both = wide[0:8]
            for g in range(1, RJ // 8):
                both = both + wide[8 * g:8 * g + 8]
            out_ref[il, :, third * LANES * VB:(third + 1) * LANES * VB] = (
                both[0:NJ] + both[NJ:2 * NJ]
            ).astype(BF16)


def store(d):
    return pl.pallas_call(
        store_kernel,
        in_specs=[pl.BlockSpec(memory_space=pltpu.VMEM)],
        out_specs=pl.BlockSpec(memory_space=pltpu.VMEM),
        out_shape=jax.ShapeDtypeStruct((IL, NJ, Q * VB * VB), BF16),
        compiler_params=pltpu.CompilerParams(vmem_limit_bytes=32 * MIB),
        cost_estimate=pl.CostEstimate(
            flops=2 * IL * THIRDS * RJ * LANES * LANES * VB,
            bytes_accessed=MIB,
            transcendentals=0,
        ),
        name="store",
    )(d)


def kept_columns(screen):
    row = lax.dynamic_slice(screen, (lax.axis_index("occ"), 0), (1, screen.shape[1]))[0]
    tiles = jnp.arange(row.shape[0], dtype=jnp.int32)
    on = row != 0
    first = jnp.min(jnp.where(on, tiles, row.shape[0] - 1))
    last = jnp.max(jnp.where(on, tiles, 0))
    width = VB // row.shape[0]
    inner = jnp.arange(width, dtype=jnp.int32)
    second = jnp.where(last > first, last * width + inner, -(10**6))
    return jnp.concatenate([first * width + inner, second])


def local(t2_tiles, w_cycle, screen):
    chosen = kept_columns(screen)
    x = jnp.transpose(t2_tiles, (1, 2, 0, 3)).reshape(BO * NI, Q * VB * VB)
    w = jnp.transpose(w_cycle, (0, 2, 1, 3)).reshape(BO * RJ, Q * VB)
    w_part = lax.all_to_all(relay_integrals(chosen, w), "z", 0, 0, tiled=True)
    w_all = lax.all_gather(w_part, ("occ", "y"), axis=0, tiled=False)
    w_all = w_all.reshape(ON, YN, ZN * RJ, KW)
    a = lax.all_to_all(relay_amplitudes(chosen, x), ("occ", "y"), 0, 0, tiled=True)
    part = contract(w_all, a.reshape(ON * KW, WIDE))
    mine = lax.psum_scatter(part, "z", scatter_dimension=0, tiled=True)
    d = mine.reshape(YN, RJ, WIDE).astype(BF16)
    d = lax.all_to_all(d, "y", 0, 0, tiled=True)
    return store(d).reshape(IL, NJ, 1, Q * VB * VB)


def solution(mesh):
    fine = Mesh(mesh.devices.reshape(ON, ZN, YN), ("occ", "z", "y"))
    vir = ("z", "y")
    placed = (P(None, "occ", vir, None), P("occ", None, vir, None), P())
    return jax.shard_map(
        local, mesh=fine, in_specs=placed, out_specs=P("occ", None, vir, None), check_vma=False
    )
```

```python
import jax
import jax.numpy as jnp
from jax import lax
from jax.experimental import pallas as pl
from jax.experimental.pallas import tpu as pltpu
from jax.sharding import Mesh, PartitionSpec as P

BF16 = jnp.bfloat16
F32 = jnp.float32
MIB = 1024 * 1024
BO = 12
VB = 12
Q = 32
ZN = 8
YN = 4
ON = 8
KEPT = 8
NI = 72
IL = 9
NJ = 4
LANES = 128
THIRDS = 3
UNITS = 7
CUTS = (0, 7)
RJ = VB * NJ
KSRC = BO * KEPT
KW = YN * KSRC


def kept_columns(screen_ref):
    o = lax.axis_index("occ")
    tiles = screen_ref.shape[0]
    width = VB // tiles
    first = jnp.int32(tiles - 1)
    last = jnp.int32(0)
    for tile in range(tiles):
        last = jnp.where(screen_ref[tile, o] != 0, tile, last)
        back = tiles - 1 - tile
        first = jnp.where(screen_ref[back, o] != 0, back, first)
    second = jnp.where(last > first, last * width, -(10**6))
    return [first * width + s for s in range(width)] + [second + s for s in range(width)]


def chunk_of(unit):
    y, slot = unit // UNITS, unit % UNITS
    chunk = max(c for c in range(len(CUTS) - 1) if CUTS[c] <= slot)
    return y, chunk, slot - CUTS[chunk]


def amplitude_kernel(screen_ref, x_ref, *rest):
    out_refs, pick_ref, rows_ref = rest[:-2], rest[-2], rest[-1]
    third = pl.program_id(0)

    @pl.when(third == 0)
    def _():
        row = lax.broadcasted_iota(jnp.int32, (LANES * VB, LANES), 0)
        col = lax.broadcasted_iota(jnp.int32, (LANES * VB, LANES), 1)
        offset = row - col * VB
        for s, column in enumerate(kept_columns(screen_ref)):
            pick_ref[:, s * LANES:(s + 1) * LANES] = jnp.where(offset == column, 1.0, 0.0).astype(
                BF16
            )
        y, chunk, place = chunk_of(YN * UNITS - 1)
        for o in range(ON):
            out_refs[chunk][o * YN + y, :, place * LANES:(place + 1) * LANES] = jnp.zeros(
                (KSRC, LANES), BF16
            )

    for pair in range(KEPT // 2):
        picked = jnp.dot(
            x_ref[...],
            pick_ref[:, pair * 2 * LANES:(pair + 1) * 2 * LANES],
            preferred_element_type=F32,
        )
        for half in range(2):
            rows_ref[pl.ds(2 * pair + half, BO * NI, stride=KEPT), :] = picked[
                :, half * LANES:(half + 1) * LANES
            ]

    for now in range(THIRDS):

        @pl.when(third == now)
        def _():
            def put(kp, carry):
                rows = pl.ds(pl.multiple_of(kp * 2 * KEPT, 2 * KEPT), 2 * KEPT)
                for i in range(NI):
                    y, chunk, place = chunk_of(now * IL + i % IL)
                    low = pl.multiple_of((2 * kp * NI + i) * KEPT, KEPT)
                    high = pl.multiple_of(((2 * kp + 1) * NI + i) * KEPT, KEPT)
                    tile = jnp.concatenate(
                        [rows_ref[pl.ds(low, KEPT), :], rows_ref[pl.ds(high, KEPT), :]], axis=0
                    ).astype(BF16)
                    out_refs[chunk][
                        (i // IL) * YN + y, rows, place * LANES:(place + 1) * LANES
                    ] = tile
                return carry

            lax.fori_loop(0, BO // 2, put, 0)


def relay_amplitudes(screen, x):
    shapes = [
        (ON * YN, KSRC, (high - low) * LANES) for low, high in zip(CUTS[:-1], CUTS[1:], strict=True)
    ]
    return pl.pallas_call(
        amplitude_kernel,
        grid=(THIRDS,),
        in_specs=[
            pl.BlockSpec(memory_space=pltpu.SMEM),
            pl.BlockSpec((BO * NI, LANES * VB), lambda t: (0, t)),
        ],
        out_specs=[pl.BlockSpec(shape, lambda t: (0, 0, 0)) for shape in shapes],
        out_shape=[jax.ShapeDtypeStruct(shape, BF16) for shape in shapes],
        scratch_shapes=[
            pltpu.VMEM((LANES * VB, KEPT * LANES), BF16),
            pltpu.VMEM((BO * NI * KEPT, LANES), F32),
        ],
        compiler_params=pltpu.CompilerParams(vmem_limit_bytes=60 * MIB),
        cost_estimate=pl.CostEstimate(
            flops=2 * BO * NI * THIRDS * LANES * VB * KEPT * LANES,
            bytes_accessed=14 * MIB,
            transcendentals=0,
        ),
        name="relay_amplitudes",
    )(screen, x)


def integral_kernel(screen_ref, w_ref, out_ref, sum_ref):
    col = lax.broadcasted_iota(jnp.int32, (8, KW), 1)
    y_of = jnp.zeros((8, KW), jnp.int32)
    for y in range(1, YN):
        y_of = jnp.where(col >= y * KSRC, y, y_of)
    inner = col - y_of * KSRC
    wanted = jnp.full((8, KW), -(10**6), jnp.int32)
    for s, column in enumerate(kept_columns(screen_ref)):
        wanted = jnp.where(inner == s, y_of * VB + column, wanted)
    row = lax.broadcasted_iota(jnp.int32, (Q * VB, KW), 0)
    offset = row - wanted[0:1]
    w = w_ref[...]
    for z in range(ZN):
        pick = jnp.where(offset == z * YN * VB, 1.0, 0.0).astype(BF16)
        sum_ref[...] = jnp.dot(w, pick, preferred_element_type=F32)
        total = sum_ref[0:RJ, :]
        for k in range(1, BO):
            total = total + pltpu.roll(sum_ref[k * RJ:(k + 1) * RJ, :], k * KEPT, 1)
        out_ref[z * RJ:(z + 1) * RJ, :] = total.astype(BF16)


def relay_integrals(screen, w):
    return pl.pallas_call(
        integral_kernel,
        in_specs=[
            pl.BlockSpec(memory_space=pltpu.SMEM),
            pl.BlockSpec(memory_space=pltpu.VMEM),
        ],
        out_specs=pl.BlockSpec(memory_space=pltpu.VMEM),
        out_shape=jax.ShapeDtypeStruct((ZN * RJ, KW), BF16),
        scratch_shapes=[
            pltpu.VMEM((BO * RJ, KW), F32),
        ],
        compiler_params=pltpu.CompilerParams(vmem_limit_bytes=16 * MIB),
        cost_estimate=pl.CostEstimate(
            flops=2 * BO * RJ * Q * VB * ZN * KW, bytes_accessed=MIB, transcendentals=0
        ),
        name="relay_integrals",
    )(screen, w)


def contract_kernel(w_ref, a_ref, out_ref):
    left = jnp.concatenate([w_ref[o, 0] for o in range(ON)], axis=1)
    product = jnp.dot(left, a_ref[...], preferred_element_type=F32)
    out_ref[...] = product.reshape(ZN, RJ, out_ref.shape[2])


def contract(w, a):
    wide = a.shape[1]
    return pl.pallas_call(
        contract_kernel,
        grid=(YN,),
        in_specs=[
            pl.BlockSpec((ON, 1, ZN * RJ, KW), lambda y: (0, y, 0, 0)),
            pl.BlockSpec((ON * KW, wide), lambda y: (0, 0), pipeline_mode=pl.Buffered(1)),
        ],
        out_specs=pl.BlockSpec((ZN, RJ, wide), lambda y: (0, y, 0)),
        out_shape=jax.ShapeDtypeStruct((ZN, YN * RJ, wide), F32),
        compiler_params=pltpu.CompilerParams(vmem_limit_bytes=60 * MIB),
        cost_estimate=pl.CostEstimate(
            flops=2 * YN * ZN * RJ * ON * KW * wide, bytes_accessed=20 * MIB, transcendentals=0
        ),
        name="contract",
    )(w, a)


def store_kernel(*refs):
    d_refs, out_ref = refs[:-1], refs[-1]
    row = lax.broadcasted_iota(jnp.int32, (LANES, LANES * VB), 0)
    col = lax.broadcasted_iota(jnp.int32, (LANES, LANES * VB), 1)
    spread = jnp.where(col // VB == row, 1.0, 0.0).astype(BF16)
    place = lax.broadcasted_iota(jnp.int32, (RJ, LANES * VB), 0) // NJ
    minor = lax.broadcasted_iota(jnp.int32, (RJ, LANES * VB), 1) % VB
    own = place == minor
    for il in range(IL):
        for third in range(THIRDS):
            unit = third * IL + il
            y, chunk, slot = chunk_of(unit)
            piece = d_refs[chunk][y, :, slot * LANES:(slot + 1) * LANES]
            wide = jnp.dot(piece, spread, preferred_element_type=F32)
            wide = jnp.where(own, wide, 0.0)
            both = wide[0:8]
            for g in range(1, RJ // 8):
                both = both + wide[8 * g:8 * g + 8]
            out_ref[il, :, third * LANES * VB:(third + 1) * LANES * VB] = (
                both[0:NJ] + both[NJ:2 * NJ]
            ).astype(BF16)


def store(parts):
    return pl.pallas_call(
        store_kernel,
        in_specs=[pl.BlockSpec(memory_space=pltpu.VMEM)] * len(parts),
        out_specs=pl.BlockSpec(memory_space=pltpu.VMEM),
        out_shape=jax.ShapeDtypeStruct((IL, NJ, Q * VB * VB), BF16),
        compiler_params=pltpu.CompilerParams(vmem_limit_bytes=16 * MIB),
        cost_estimate=pl.CostEstimate(
            flops=2 * IL * THIRDS * RJ * LANES * LANES * VB,
            bytes_accessed=MIB,
            transcendentals=0,
        ),
        name="store",
    )(*parts)


def local(t2_tiles, w_cycle, screen):
    tiles = screen.T
    x = jnp.transpose(t2_tiles, (1, 2, 0, 3)).reshape(BO * NI, Q * VB * VB)
    w = jnp.transpose(w_cycle, (0, 2, 1, 3)).reshape(BO * RJ, Q * VB)
    w_part = relay_integrals(tiles, w).reshape(ZN, RJ, KW)
    w_part = lax.all_to_all(w_part, "z", 0, 0, tiled=True)
    w_part, sends = lax.optimization_barrier((w_part, relay_amplitudes(tiles, x)))
    w_all = lax.all_gather(w_part, ("occ", "y"), axis=0, tiled=False)
    w_all = w_all.reshape(ON, YN, ZN * RJ, KW)
    done = []
    part = None
    for send in sends:
        if part is not None:
            send, part = lax.optimization_barrier((send, part))
            done[-1] = part
        a = lax.all_to_all(send, ("occ", "y"), 0, 0, tiled=True)
        part = contract(w_all, a.reshape(ON * KW, a.shape[2]))
        done.append(part)
    results = []
    for part in done:
        mine = lax.psum_scatter(part, "z", scatter_dimension=0, tiled=True)
        d = mine.reshape(YN, RJ, mine.shape[2]).astype(BF16)
        results.append(lax.all_to_all(d, "y", 0, 0, tiled=True))
    return store(results).reshape(IL, NJ, 1, Q * VB * VB)


def solution(mesh):
    fine = Mesh(mesh.devices.reshape(ON, ZN, YN), ("occ", "z", "y"))
    vir = ("z", "y")
    placed = (P(None, "occ", vir, None), P("occ", None, vir, None), P())
    return jax.shard_map(
        local, mesh=fine, in_specs=placed, out_specs=P("occ", None, vir, None), check_vma=False
    )
```

```python
import jax
import jax.numpy as jnp
from jax import lax
from jax.experimental import pallas as pl
from jax.experimental.pallas import tpu as pltpu
from jax.sharding import Mesh, PartitionSpec as P

BF16 = jnp.bfloat16
F32 = jnp.float32
MIB = 1024 * 1024
BO = 12
VB = 12
Q = 32
ZN = 8
YN = 4
ON = 8
KEPT = 8
NI = 72
IL = 9
NJ = 4
LANES = 128
HALF = LANES // 2
THIRDS = 3
UNITS = 7
WIDE = UNITS * LANES
RJ = VB * NJ
KSRC = BO * KEPT
KW = YN * KSRC


def kept_columns(screen_ref):
    o = lax.axis_index("occ")
    tiles = screen_ref.shape[0]
    width = VB // tiles
    first = jnp.int32(tiles - 1)
    last = jnp.int32(0)
    for tile in range(tiles):
        last = jnp.where(screen_ref[tile, o] != 0, tile, last)
        back = tiles - 1 - tile
        first = jnp.where(screen_ref[back, o] != 0, back, first)
    second = jnp.where(last > first, last * width, -(10**6))
    return [first * width + s for s in range(width)] + [second + s for s in range(width)]


def amplitude_kernel(screen_ref, x_ref, out_ref, pick_ref, rows_ref):
    third = pl.program_id(0)

    @pl.when(third == 0)
    def _():
        row = lax.broadcasted_iota(jnp.int32, (HALF * VB, LANES), 0)
        col = lax.broadcasted_iota(jnp.int32, (HALF * VB, LANES), 1)
        upper = col >= HALF
        offset = row - jnp.where(upper, col - HALF, col) * VB
        columns = kept_columns(screen_ref)
        for pair in range(KEPT // 2):
            even, odd = columns[2 * pair], columns[2 * pair + 1]
            at = slice(pair * LANES, (pair + 1) * LANES)
            pick_ref[0, :, at] = jnp.where(
                offset == jnp.where(upper, odd, even), 1.0, 0.0
            ).astype(BF16)
            pick_ref[1, :, at] = jnp.where(
                offset == jnp.where(upper, even, odd), 1.0, 0.0
            ).astype(BF16)
        for o in range(ON):
            out_ref[o * YN + YN - 1, :, (UNITS - 1) * LANES:] = jnp.zeros((KSRC, LANES), BF16)

    low, high = (
        jnp.dot(
            x_ref[:, half * HALF * VB:(half + 1) * HALF * VB],
            pick_ref[half],
            preferred_element_type=F32,
        )
        for half in range(2)
    )
    lower = lax.broadcasted_iota(jnp.int32, (BO * NI, LANES), 1) < HALF
    for pair in range(KEPT // 2):
        at = slice(pair * LANES, (pair + 1) * LANES)
        even = jnp.where(lower, low[:, at], high[:, at])
        odd = jnp.where(lower, high[:, at], low[:, at])
        rows_ref[pl.ds(2 * pair, BO * NI, stride=KEPT), :] = even
        rows_ref[pl.ds(2 * pair + 1, BO * NI, stride=KEPT), :] = pltpu.roll(odd, HALF, 1)

    for now in range(THIRDS):

        @pl.when(third == now)
        def _():
            def put(kp, carry):
                rows = pl.ds(pl.multiple_of(kp * 2 * KEPT, 2 * KEPT), 2 * KEPT)
                for i in range(NI):
                    y, place = divmod(now * IL + i % IL, UNITS)
                    low = pl.multiple_of((2 * kp * NI + i) * KEPT, KEPT)
                    high = pl.multiple_of(((2 * kp + 1) * NI + i) * KEPT, KEPT)
                    tile = jnp.concatenate(
                        [rows_ref[pl.ds(low, KEPT), :], rows_ref[pl.ds(high, KEPT), :]], axis=0
                    ).astype(BF16)
                    out_ref[(i // IL) * YN + y, rows, place * LANES:(place + 1) * LANES] = tile
                return carry

            lax.fori_loop(0, BO // 2, put, 0)


def relay_amplitudes(screen, x):
    shape = (ON * YN, KSRC, WIDE)
    return pl.pallas_call(
        amplitude_kernel,
        grid=(THIRDS,),
        in_specs=[
            pl.BlockSpec(memory_space=pltpu.SMEM),
            pl.BlockSpec((BO * NI, LANES * VB), lambda t: (0, t)),
        ],
        out_specs=pl.BlockSpec(shape, lambda t: (0, 0, 0)),
        out_shape=jax.ShapeDtypeStruct(shape, BF16),
        scratch_shapes=[
            pltpu.VMEM((2, HALF * VB, KEPT * HALF), BF16),
            pltpu.VMEM((BO * NI * KEPT, LANES), F32),
        ],
        compiler_params=pltpu.CompilerParams(vmem_limit_bytes=60 * MIB),
        cost_estimate=pl.CostEstimate(
            flops=2 * BO * NI * THIRDS * LANES * VB * KEPT * HALF,
            bytes_accessed=14 * MIB,
            transcendentals=0,
        ),
        name="relay_amplitudes",
    )(screen, x)


def integral_kernel(screen_ref, w_ref, out_ref, sum_ref):
    col = lax.broadcasted_iota(jnp.int32, (8, KW), 1)
    y_of = jnp.zeros((8, KW), jnp.int32)
    for y in range(1, YN):
        y_of = jnp.where(col >= y * KSRC, y, y_of)
    inner = col - y_of * KSRC
    wanted = jnp.full((8, KW), -(10**6), jnp.int32)
    for s, column in enumerate(kept_columns(screen_ref)):
        wanted = jnp.where(inner == s, y_of * VB + column, wanted)
    row = lax.broadcasted_iota(jnp.int32, (Q * VB, KW), 0)
    offset = row - wanted[0:1]
    w = w_ref[...]
    for z in range(ZN):
        pick = jnp.where(offset == z * YN * VB, 1.0, 0.0).astype(BF16)
        sum_ref[...] = jnp.dot(w, pick, preferred_element_type=F32)
        total = sum_ref[0:RJ, :]
        for k in range(1, BO):
            total = total + pltpu.roll(sum_ref[k * RJ:(k + 1) * RJ, :], k * KEPT, 1)
        out_ref[z * RJ:(z + 1) * RJ, :] = total.astype(BF16)


def relay_integrals(screen, w):
    return pl.pallas_call(
        integral_kernel,
        in_specs=[
            pl.BlockSpec(memory_space=pltpu.SMEM),
            pl.BlockSpec(memory_space=pltpu.VMEM),
        ],
        out_specs=pl.BlockSpec(memory_space=pltpu.VMEM),
        out_shape=jax.ShapeDtypeStruct((ZN * RJ, KW), BF16),
        scratch_shapes=[
            pltpu.VMEM((BO * RJ, KW), F32),
        ],
        compiler_params=pltpu.CompilerParams(vmem_limit_bytes=16 * MIB),
        cost_estimate=pl.CostEstimate(
            flops=2 * BO * RJ * Q * VB * ZN * KW, bytes_accessed=MIB, transcendentals=0
        ),
        name="relay_integrals",
    )(screen, w)


def contract_kernel(w_ref, a_ref, out_ref):
    left = jnp.concatenate([w_ref[o, 0] for o in range(ON)], axis=1)
    product = jnp.dot(left, a_ref[...], preferred_element_type=F32)
    out_ref[...] = product.reshape(ZN, RJ, WIDE)


def contract(w, a):
    return pl.pallas_call(
        contract_kernel,
        grid=(YN,),
        in_specs=[
            pl.BlockSpec((ON, 1, ZN * RJ, KW), lambda y: (0, y, 0, 0)),
            pl.BlockSpec((ON * KW, WIDE), lambda y: (0, 0), pipeline_mode=pl.Buffered(1)),
        ],
        out_specs=pl.BlockSpec((ZN, RJ, WIDE), lambda y: (0, y, 0)),
        out_shape=jax.ShapeDtypeStruct((ZN, YN * RJ, WIDE), F32),
        compiler_params=pltpu.CompilerParams(vmem_limit_bytes=60 * MIB),
        cost_estimate=pl.CostEstimate(
            flops=2 * YN * ZN * RJ * ON * KW * WIDE, bytes_accessed=20 * MIB, transcendentals=0
        ),
        name="contract",
    )(w, a)


def store_kernel(d_ref, out_ref):
    row = lax.broadcasted_iota(jnp.int32, (LANES, LANES * VB), 0)
    col = lax.broadcasted_iota(jnp.int32, (LANES, LANES * VB), 1)
    spread = jnp.where(col // VB == row, 1.0, 0.0).astype(BF16)
    place = lax.broadcasted_iota(jnp.int32, (RJ, LANES * VB), 0) // NJ
    minor = lax.broadcasted_iota(jnp.int32, (RJ, LANES * VB), 1) % VB
    own = place == minor
    for il in range(IL):
        for third in range(THIRDS):
            unit = third * IL + il
            y, slot = divmod(unit, UNITS)
            piece = d_ref[y, :, slot * LANES:(slot + 1) * LANES]
            wide = jnp.dot(piece, spread, preferred_element_type=F32)
            wide = jnp.where(own, wide, 0.0)
            both = wide[0:8]
            for g in range(1, RJ // 8):
                both = both + wide[8 * g:8 * g + 8]
            out_ref[il, :, third * LANES * VB:(third + 1) * LANES * VB] = (
                both[0:NJ] + both[NJ:2 * NJ]
            ).astype(BF16)


def store(d):
    return pl.pallas_call(
        store_kernel,
        in_specs=[pl.BlockSpec(memory_space=pltpu.VMEM)],
        out_specs=pl.BlockSpec(memory_space=pltpu.VMEM),
        out_shape=jax.ShapeDtypeStruct((IL, NJ, Q * VB * VB), BF16),
        compiler_params=pltpu.CompilerParams(vmem_limit_bytes=16 * MIB),
        cost_estimate=pl.CostEstimate(
            flops=2 * IL * THIRDS * RJ * LANES * LANES * VB,
            bytes_accessed=MIB,
            transcendentals=0,
        ),
        name="store",
    )(d)


def local(t2_tiles, w_cycle, screen):
    tiles = screen.T
    x = jnp.transpose(t2_tiles, (1, 2, 0, 3)).reshape(BO * NI, Q * VB * VB)
    w = jnp.transpose(w_cycle, (0, 2, 1, 3)).reshape(BO * RJ, Q * VB)
    w_part = relay_integrals(tiles, w).reshape(ZN, RJ, KW)
    w_part = lax.all_to_all(w_part, "z", 0, 0, tiled=True)
    w_part, send = lax.optimization_barrier((w_part, relay_amplitudes(tiles, x)))
    w_all = lax.all_gather(w_part, ("occ", "y"), axis=0, tiled=False)
    w_all = w_all.reshape(ON, YN, ZN * RJ, KW)
    a = lax.all_to_all(send, ("occ", "y"), 0, 0, tiled=True).reshape(ON * KW, WIDE)
    part = contract(w_all, a)
    mine = lax.psum_scatter(part, "z", scatter_dimension=0, tiled=True)
    d = mine.reshape(YN, RJ, WIDE).astype(BF16)
    d = lax.all_to_all(d, "y", 0, 0, tiled=True)
    return store(d).reshape(IL, NJ, 1, Q * VB * VB)


def solution(mesh):
    fine = Mesh(mesh.devices.reshape(ON, ZN, YN), ("occ", "z", "y"))
    vir = ("z", "y")
    placed = (P(None, "occ", vir, None), P("occ", None, vir, None), P())
    return jax.shard_map(
        local, mesh=fine, in_specs=placed, out_specs=P("occ", None, vir, None), check_vma=False
    )
```

```python
import jax
import jax.numpy as jnp
from jax import lax
from jax.experimental import pallas as pl
from jax.experimental.pallas import tpu as pltpu
from jax.sharding import Mesh, PartitionSpec as P

BF16 = jnp.bfloat16
F32 = jnp.float32
MIB = 1024 * 1024
BO = 12
VB = 12
Q = 32
ZN = 8
YN = 4
ON = 8
KEPT = 8
NI = 72
IL = 9
NJ = 4
LANES = 128
HALF = LANES // 2
THIRDS = 3
UNITS = 7
WIDE = UNITS * LANES
RJ = VB * NJ
KSRC = BO * KEPT
KW = YN * KSRC


def kept_columns(screen_ref):
    o = lax.axis_index("occ")
    tiles = screen_ref.shape[0]
    width = VB // tiles
    first = jnp.int32(tiles - 1)
    last = jnp.int32(0)
    for tile in range(tiles):
        last = jnp.where(screen_ref[tile, o] != 0, tile, last)
        back = tiles - 1 - tile
        first = jnp.where(screen_ref[back, o] != 0, back, first)
    second = jnp.where(last > first, last * width, -(10**6))
    return [first * width + s for s in range(width)] + [second + s for s in range(width)]


def amplitude_kernel(screen_ref, x_ref, out_ref, pick_ref, rows_ref):
    third = pl.program_id(0)

    @pl.when(third == 0)
    def _():
        row = lax.broadcasted_iota(jnp.int32, (HALF * VB, LANES), 0)
        col = lax.broadcasted_iota(jnp.int32, (HALF * VB, LANES), 1)
        upper = col >= HALF
        offset = row - jnp.where(upper, col - HALF, col) * VB
        columns = kept_columns(screen_ref)
        for pair in range(KEPT // 2):
            even, odd = columns[2 * pair], columns[2 * pair + 1]
            at = slice(pair * LANES, (pair + 1) * LANES)
            pick_ref[0, :, at] = jnp.where(
                offset == jnp.where(upper, odd, even), 1.0, 0.0
            ).astype(BF16)
            pick_ref[1, :, at] = jnp.where(
                offset == jnp.where(upper, even, odd), 1.0, 0.0
            ).astype(BF16)
        for o in range(ON):
            out_ref[o * YN + YN - 1, :, (UNITS - 1) * LANES:] = jnp.zeros((KSRC, LANES), BF16)

    low, high = (
        jnp.dot(
            x_ref[:, half * HALF * VB:(half + 1) * HALF * VB],
            pick_ref[half],
            preferred_element_type=F32,
        )
        for half in range(2)
    )
    lower = lax.broadcasted_iota(jnp.int32, (BO * NI, LANES), 1) < HALF
    for pair in range(KEPT // 2):
        at = slice(pair * LANES, (pair + 1) * LANES)
        even = jnp.where(lower, low[:, at], high[:, at])
        odd = jnp.where(lower, high[:, at], low[:, at])
        rows_ref[pl.ds(2 * pair, BO * NI, stride=KEPT), :] = even
        rows_ref[pl.ds(2 * pair + 1, BO * NI, stride=KEPT), :] = pltpu.roll(odd, HALF, 1)

    for now in range(THIRDS):

        @pl.when(third == now)
        def _():
            def put(kp, carry):
                rows = pl.ds(pl.multiple_of(kp * 2 * KEPT, 2 * KEPT), 2 * KEPT)
                for i in range(NI):
                    y, place = divmod(now * IL + i % IL, UNITS)
                    low = pl.multiple_of((2 * kp * NI + i) * KEPT, KEPT)
                    high = pl.multiple_of(((2 * kp + 1) * NI + i) * KEPT, KEPT)
                    tile = jnp.concatenate(
                        [rows_ref[pl.ds(low, KEPT), :], rows_ref[pl.ds(high, KEPT), :]], axis=0
                    ).astype(BF16)
                    out_ref[(i // IL) * YN + y, rows, place * LANES:(place + 1) * LANES] = tile
                return carry

            lax.fori_loop(0, BO // 2, put, 0)


def relay_amplitudes(screen, x):
    shape = (ON * YN, KSRC, WIDE)
    return pl.pallas_call(
        amplitude_kernel,
        grid=(THIRDS,),
        in_specs=[
            pl.BlockSpec(memory_space=pltpu.SMEM),
            pl.BlockSpec((BO * NI, LANES * VB), lambda t: (0, t)),
        ],
        out_specs=pl.BlockSpec(shape, lambda t: (0, 0, 0)),
        out_shape=jax.ShapeDtypeStruct(shape, BF16),
        scratch_shapes=[
            pltpu.VMEM((2, HALF * VB, KEPT * HALF), BF16),
            pltpu.VMEM((BO * NI * KEPT + KEPT, LANES), F32),
        ],
        compiler_params=pltpu.CompilerParams(vmem_limit_bytes=60 * MIB),
        cost_estimate=pl.CostEstimate(
            flops=2 * BO * NI * THIRDS * LANES * VB * KEPT * HALF,
            bytes_accessed=14 * MIB,
            transcendentals=0,
        ),
        name="relay_amplitudes",
    )(screen, x)


def integral_kernel(screen_ref, w_ref, out_ref, sum_ref):
    col = lax.broadcasted_iota(jnp.int32, (8, KW), 1)
    y_of = jnp.zeros((8, KW), jnp.int32)
    for y in range(1, YN):
        y_of = jnp.where(col >= y * KSRC, y, y_of)
    inner = col - y_of * KSRC
    wanted = jnp.full((8, KW), -(10**6), jnp.int32)
    for s, column in enumerate(kept_columns(screen_ref)):
        wanted = jnp.where(inner == s, y_of * VB + column, wanted)
    row = lax.broadcasted_iota(jnp.int32, (2 * LANES, KW), 0)
    offset = row - wanted[0:1]
    for z in range(ZN):
        start = 0 if (z + 1) * YN * VB <= 2 * LANES else LANES
        pick = jnp.where(offset == z * YN * VB - start, 1.0, 0.0).astype(BF16)
        sum_ref[...] = jnp.dot(
            w_ref[:, start:start + 2 * LANES], pick, preferred_element_type=F32
        )
        total = sum_ref[0:RJ, :]
        for k in range(1, BO):
            total = total + pltpu.roll(sum_ref[k * RJ:(k + 1) * RJ, :], k * KEPT, 1)
        out_ref[z * RJ:(z + 1) * RJ, :] = total.astype(BF16)


def relay_integrals(screen, w):
    return pl.pallas_call(
        integral_kernel,
        in_specs=[
            pl.BlockSpec(memory_space=pltpu.SMEM),
            pl.BlockSpec(memory_space=pltpu.VMEM),
        ],
        out_specs=pl.BlockSpec(memory_space=pltpu.VMEM),
        out_shape=jax.ShapeDtypeStruct((ZN * RJ, KW), BF16),
        scratch_shapes=[
            pltpu.VMEM((BO * RJ, KW), F32),
        ],
        compiler_params=pltpu.CompilerParams(vmem_limit_bytes=16 * MIB),
        cost_estimate=pl.CostEstimate(
            flops=2 * BO * RJ * Q * VB * ZN * KW, bytes_accessed=MIB, transcendentals=0
        ),
        name="relay_integrals",
    )(screen, w)


def contract_kernel(w_ref, a_ref, out_ref):
    left = jnp.concatenate([w_ref[o, 0] for o in range(ON)], axis=1)
    product = jnp.dot(left, a_ref[...], preferred_element_type=F32)
    out_ref[...] = product.reshape(ZN, RJ, WIDE)


def contract(w, a):
    return pl.pallas_call(
        contract_kernel,
        grid=(YN,),
        in_specs=[
            pl.BlockSpec((ON, 1, ZN * RJ, KW), lambda y: (0, y, 0, 0)),
            pl.BlockSpec((ON * KW, WIDE), lambda y: (0, 0), pipeline_mode=pl.Buffered(1)),
        ],
        out_specs=pl.BlockSpec((ZN, RJ, WIDE), lambda y: (0, y, 0)),
        out_shape=jax.ShapeDtypeStruct((ZN, YN * RJ, WIDE), F32),
        compiler_params=pltpu.CompilerParams(vmem_limit_bytes=60 * MIB),
        cost_estimate=pl.CostEstimate(
            flops=2 * YN * ZN * RJ * ON * KW * WIDE, bytes_accessed=20 * MIB, transcendentals=0
        ),
        name="contract",
    )(w, a)


def store_kernel(d_ref, out_ref):
    row = lax.broadcasted_iota(jnp.int32, (LANES, LANES * VB), 0)
    col = lax.broadcasted_iota(jnp.int32, (LANES, LANES * VB), 1)
    spread = jnp.where(col // VB == row, 1.0, 0.0).astype(BF16)
    place = lax.broadcasted_iota(jnp.int32, (RJ, LANES * VB), 0) // NJ
    minor = lax.broadcasted_iota(jnp.int32, (RJ, LANES * VB), 1) % VB
    own = place == minor
    for il in range(IL):
        for third in range(THIRDS):
            unit = third * IL + il
            y, slot = divmod(unit, UNITS)
            piece = d_ref[y, :, slot * LANES:(slot + 1) * LANES]
            wide = jnp.dot(piece, spread, preferred_element_type=F32)
            wide = jnp.where(own, wide, 0.0)
            both = wide[0:8]
            for g in range(1, RJ // 8):
                both = both + wide[8 * g:8 * g + 8]
            out_ref[il, :, third * LANES * VB:(third + 1) * LANES * VB] = (
                both[0:NJ] + both[NJ:2 * NJ]
            ).astype(BF16)


def store(d):
    return pl.pallas_call(
        store_kernel,
        in_specs=[pl.BlockSpec(memory_space=pltpu.VMEM)],
        out_specs=pl.BlockSpec(memory_space=pltpu.VMEM),
        out_shape=jax.ShapeDtypeStruct((IL, NJ, Q * VB * VB), BF16),
        compiler_params=pltpu.CompilerParams(vmem_limit_bytes=16 * MIB),
        cost_estimate=pl.CostEstimate(
            flops=2 * IL * THIRDS * RJ * LANES * LANES * VB,
            bytes_accessed=MIB,
            transcendentals=0,
        ),
        name="store",
    )(d)


def local(t2_tiles, w_cycle, screen):
    tiles = screen.T
    x = jnp.transpose(t2_tiles, (1, 2, 0, 3)).reshape(BO * NI, Q * VB * VB)
    w = jnp.transpose(w_cycle, (0, 2, 1, 3)).reshape(BO * RJ, Q * VB)
    w_part = relay_integrals(tiles, w).reshape(ZN, RJ, KW)
    w_part = lax.all_to_all(w_part, "z", 0, 0, tiled=True)
    w_part, send = lax.optimization_barrier((w_part, relay_amplitudes(tiles, x)))
    w_all = lax.all_gather(w_part, ("occ", "y"), axis=0, tiled=False)
    w_all = w_all.reshape(ON, YN, ZN * RJ, KW)
    a = lax.all_to_all(send, ("occ", "y"), 0, 0, tiled=True).reshape(ON * KW, WIDE)
    part = contract(w_all, a)
    mine = lax.psum_scatter(part, "z", scatter_dimension=0, tiled=True)
    d = mine.reshape(YN, RJ, WIDE).astype(BF16)
    d = lax.all_to_all(d, "y", 0, 0, tiled=True)
    return store(d).reshape(IL, NJ, 1, Q * VB * VB)


def solution(mesh):
    fine = Mesh(mesh.devices.reshape(ON, ZN, YN), ("occ", "z", "y"))
    vir = ("z", "y")
    placed = (P(None, "occ", vir, None), P("occ", None, vir, None), P())
    return jax.shard_map(
        local, mesh=fine, in_specs=placed, out_specs=P("occ", None, vir, None), check_vma=False
    )
```

```python
import jax
import jax.numpy as jnp
from jax import lax
from jax.experimental import pallas as pl
from jax.experimental.pallas import tpu as pltpu
from jax.sharding import Mesh, PartitionSpec as P

BF16 = jnp.bfloat16
F32 = jnp.float32
MIB = 1024 * 1024
BO = 12
VB = 12
Q = 32
ZN = 8
YN = 4
ON = 8
KEPT = 8
NI = 72
IL = 9
NJ = 4
LANES = 128
HALF = LANES // 2
THIRDS = 3
UNITS = 7
WIDE = UNITS * LANES
RJ = VB * NJ
KSRC = BO * KEPT
KW = YN * KSRC


def kept_columns(screen_ref):
    o = lax.axis_index("occ")
    tiles = screen_ref.shape[0]
    width = VB // tiles
    first = jnp.int32(tiles - 1)
    last = jnp.int32(0)
    for tile in range(tiles):
        last = jnp.where(screen_ref[tile, o] != 0, tile, last)
        back = tiles - 1 - tile
        first = jnp.where(screen_ref[back, o] != 0, back, first)
    second = jnp.where(last > first, last * width, -(10**6))
    return [first * width + s for s in range(width)] + [second + s for s in range(width)]


def amplitude_kernel(screen_ref, x_ref, out_ref, pick_ref, rows_ref):
    third = pl.program_id(0)

    @pl.when(third == 0)
    def _():
        row = lax.broadcasted_iota(jnp.int32, (HALF * VB, LANES), 0)
        col = lax.broadcasted_iota(jnp.int32, (HALF * VB, LANES), 1)
        upper = col >= HALF
        offset = row - jnp.where(upper, col - HALF, col) * VB
        columns = kept_columns(screen_ref)
        for pair in range(KEPT // 2):
            even, odd = columns[2 * pair], columns[2 * pair + 1]
            at = slice(pair * LANES, (pair + 1) * LANES)
            pick_ref[0, :, at] = jnp.where(
                offset == jnp.where(upper, odd, even), 1.0, 0.0
            ).astype(BF16)
            pick_ref[1, :, at] = jnp.where(
                offset == jnp.where(upper, even, odd), 1.0, 0.0
            ).astype(BF16)
        for o in range(ON):
            out_ref[o * YN + YN - 1, :, (UNITS - 1) * LANES:] = jnp.zeros((KSRC, LANES), BF16)

    low, high = (
        jnp.dot(
            x_ref[:, half * HALF * VB:(half + 1) * HALF * VB],
            pick_ref[half],
            preferred_element_type=F32,
        )
        for half in range(2)
    )
    lower = lax.broadcasted_iota(jnp.int32, (BO * NI, LANES), 1) < HALF
    for pair in range(KEPT // 2):
        at = slice(pair * LANES, (pair + 1) * LANES)
        even = jnp.where(lower, low[:, at], high[:, at])
        odd = jnp.where(lower, high[:, at], low[:, at])
        rows_ref[pl.ds(2 * pair, BO * NI, stride=KEPT), :] = even
        rows_ref[pl.ds(2 * pair + 1, BO * NI, stride=KEPT), :] = pltpu.roll(odd, HALF, 1)

    for now in range(THIRDS):

        @pl.when(third == now)
        def _():
            def put(kp, carry):
                rows = pl.ds(pl.multiple_of(kp * 2 * KEPT, 2 * KEPT), 2 * KEPT)
                for i in range(NI):
                    y, place = divmod(now * IL + i % IL, UNITS)
                    low = pl.multiple_of((2 * kp * NI + i) * KEPT, KEPT)
                    high = pl.multiple_of(((2 * kp + 1) * NI + i) * KEPT, KEPT)
                    tile = jnp.concatenate(
                        [rows_ref[pl.ds(low, KEPT), :], rows_ref[pl.ds(high, KEPT), :]], axis=0
                    ).astype(BF16)
                    out_ref[(i // IL) * YN + y, rows, place * LANES:(place + 1) * LANES] = tile
                return carry

            lax.fori_loop(0, BO // 2, put, 0)


def relay_amplitudes(screen, x):
    shape = (ON * YN, KSRC, WIDE)
    return pl.pallas_call(
        amplitude_kernel,
        grid=(THIRDS,),
        in_specs=[
            pl.BlockSpec(memory_space=pltpu.SMEM),
            pl.BlockSpec((BO * NI, LANES * VB), lambda t: (0, t)),
        ],
        out_specs=pl.BlockSpec(shape, lambda t: (0, 0, 0)),
        out_shape=jax.ShapeDtypeStruct(shape, BF16),
        scratch_shapes=[
            pltpu.VMEM((2, HALF * VB, KEPT * HALF), BF16),
            pltpu.VMEM((BO * NI * KEPT + KEPT, LANES), F32),
        ],
        compiler_params=pltpu.CompilerParams(vmem_limit_bytes=60 * MIB),
        cost_estimate=pl.CostEstimate(
            flops=2 * BO * NI * THIRDS * LANES * VB * KEPT * HALF,
            bytes_accessed=14 * MIB,
            transcendentals=0,
        ),
        name="relay_amplitudes",
    )(screen, x)


def integral_kernel(screen_ref, w_ref, out_ref, sum_ref):
    col = lax.broadcasted_iota(jnp.int32, (8, KW), 1)
    y_of = jnp.zeros((8, KW), jnp.int32)
    for y in range(1, YN):
        y_of = jnp.where(col >= y * KSRC, y, y_of)
    inner = col - y_of * KSRC
    wanted = jnp.full((8, KW), -(10**6), jnp.int32)
    for s, column in enumerate(kept_columns(screen_ref)):
        wanted = jnp.where(inner == s, y_of * VB + column, wanted)
    row = lax.broadcasted_iota(jnp.int32, (2 * LANES, KW), 0)
    offset = row - wanted[0:1]
    w = w_ref[...].reshape(BO * RJ, Q * VB)
    for z in range(ZN):
        start = 0 if (z + 1) * YN * VB <= 2 * LANES else LANES
        pick = jnp.where(offset == z * YN * VB - start, 1.0, 0.0).astype(BF16)
        sum_ref[...] = jnp.dot(
            w[:, start:start + 2 * LANES], pick, preferred_element_type=F32
        )
        total = sum_ref[0:RJ, :]
        for k in range(1, BO):
            total = total + pltpu.roll(sum_ref[k * RJ:(k + 1) * RJ, :], k * KEPT, 1)
        out_ref[z * RJ:(z + 1) * RJ, :] = total.astype(BF16)


def relay_integrals(screen, w):
    return pl.pallas_call(
        integral_kernel,
        in_specs=[
            pl.BlockSpec(memory_space=pltpu.SMEM),
            pl.BlockSpec(memory_space=pltpu.VMEM),
        ],
        out_specs=pl.BlockSpec(memory_space=pltpu.VMEM),
        out_shape=jax.ShapeDtypeStruct((ZN * RJ, KW), BF16),
        scratch_shapes=[
            pltpu.VMEM((BO * RJ, KW), F32),
        ],
        compiler_params=pltpu.CompilerParams(vmem_limit_bytes=62 * MIB),
        cost_estimate=pl.CostEstimate(
            flops=2 * BO * RJ * Q * VB * ZN * KW, bytes_accessed=MIB, transcendentals=0
        ),
        name="relay_integrals",
    )(screen, w)


def contract_kernel(w_ref, a_ref, out_ref):
    left = jnp.concatenate([w_ref[o, 0] for o in range(ON)], axis=1)
    product = jnp.dot(left, a_ref[...], preferred_element_type=F32)
    out_ref[...] = product.reshape(ZN, RJ, WIDE)


def contract(w, a):
    return pl.pallas_call(
        contract_kernel,
        grid=(YN,),
        in_specs=[
            pl.BlockSpec((ON, 1, ZN * RJ, KW), lambda y: (0, y, 0, 0)),
            pl.BlockSpec((ON * KW, WIDE), lambda y: (0, 0), pipeline_mode=pl.Buffered(1)),
        ],
        out_specs=pl.BlockSpec((ZN, RJ, WIDE), lambda y: (0, y, 0)),
        out_shape=jax.ShapeDtypeStruct((ZN, YN * RJ, WIDE), F32),
        compiler_params=pltpu.CompilerParams(vmem_limit_bytes=60 * MIB),
        cost_estimate=pl.CostEstimate(
            flops=2 * YN * ZN * RJ * ON * KW * WIDE, bytes_accessed=20 * MIB, transcendentals=0
        ),
        name="contract",
    )(w, a)


def store_kernel(d_ref, out_ref):
    row = lax.broadcasted_iota(jnp.int32, (LANES, LANES * VB), 0)
    col = lax.broadcasted_iota(jnp.int32, (LANES, LANES * VB), 1)
    spread = jnp.where(col // VB == row, 1.0, 0.0).astype(BF16)
    place = lax.broadcasted_iota(jnp.int32, (RJ, LANES * VB), 0) // NJ
    minor = lax.broadcasted_iota(jnp.int32, (RJ, LANES * VB), 1) % VB
    own = place == minor
    for il in range(IL):
        for third in range(THIRDS):
            unit = third * IL + il
            y, slot = divmod(unit, UNITS)
            piece = d_ref[y, :, slot * LANES:(slot + 1) * LANES]
            wide = jnp.dot(piece, spread, preferred_element_type=F32)
            wide = jnp.where(own, wide, 0.0)
            both = wide[0:8]
            for g in range(1, RJ // 8):
                both = both + wide[8 * g:8 * g + 8]
            out_ref[il, :, third * LANES * VB:(third + 1) * LANES * VB] = (
                both[0:NJ] + both[NJ:2 * NJ]
            ).astype(BF16)


def store(d):
    return pl.pallas_call(
        store_kernel,
        in_specs=[pl.BlockSpec(memory_space=pltpu.VMEM)],
        out_specs=pl.BlockSpec(memory_space=pltpu.VMEM),
        out_shape=jax.ShapeDtypeStruct((IL, NJ, Q * VB * VB), BF16),
        compiler_params=pltpu.CompilerParams(vmem_limit_bytes=16 * MIB),
        cost_estimate=pl.CostEstimate(
            flops=2 * IL * THIRDS * RJ * LANES * LANES * VB,
            bytes_accessed=MIB,
            transcendentals=0,
        ),
        name="store",
    )(d)


def local(t2_tiles, w_cycle, screen):
    tiles = screen.T
    x = jnp.transpose(t2_tiles, (1, 2, 0, 3)).reshape(BO * NI, Q * VB * VB)
    w = jnp.transpose(w_cycle, (0, 2, 1, 3)).reshape(BO * VB, NJ, Q * VB)
    w_part = relay_integrals(tiles, w).reshape(ZN, RJ, KW)
    w_part = lax.all_to_all(w_part, "z", 0, 0, tiled=True)
    w_part, send = lax.optimization_barrier((w_part, relay_amplitudes(tiles, x)))
    w_all = lax.all_gather(w_part, ("occ", "y"), axis=0, tiled=False)
    w_all = w_all.reshape(ON, YN, ZN * RJ, KW)
    a = lax.all_to_all(send, ("occ", "y"), 0, 0, tiled=True).reshape(ON * KW, WIDE)
    part = contract(w_all, a)
    mine = lax.psum_scatter(part, "z", scatter_dimension=0, tiled=True)
    d = mine.reshape(YN, RJ, WIDE).astype(BF16)
    d = lax.all_to_all(d, "y", 0, 0, tiled=True)
    return store(d).reshape(IL, NJ, 1, Q * VB * VB)


def solution(mesh):
    fine = Mesh(mesh.devices.reshape(ON, ZN, YN), ("occ", "z", "y"))
    vir = ("z", "y")
    placed = (P(None, "occ", vir, None), P("occ", None, vir, None), P())
    return jax.shard_map(
        local, mesh=fine, in_specs=placed, out_specs=P("occ", None, vir, None), check_vma=False
    )
```

```python
import jax
import jax.numpy as jnp
from jax import lax
from jax.experimental import pallas as pl
from jax.experimental.pallas import tpu as pltpu
from jax.sharding import Mesh, PartitionSpec as P

BF16 = jnp.bfloat16
F32 = jnp.float32
MIB = 1024 * 1024
BO = 12
VB = 12
Q = 32
ZN = 8
YN = 4
ON = 8
KEPT = 8
NI = 72
IL = 9
NJ = 4
LANES = 128
HALF = LANES // 2
THIRDS = 3
UNITS = 7
WIDE = UNITS * LANES
RJ = VB * NJ
KSRC = BO * KEPT
KW = YN * KSRC


def kept_columns(screen_ref):
    o = lax.axis_index("occ")
    tiles = screen_ref.shape[0]
    width = VB // tiles
    first = jnp.int32(tiles - 1)
    last = jnp.int32(0)
    for tile in range(tiles):
        last = jnp.where(screen_ref[tile, o] != 0, tile, last)
        back = tiles - 1 - tile
        first = jnp.where(screen_ref[back, o] != 0, back, first)
    second = jnp.where(last > first, last * width, -(10**6))
    return [first * width + s for s in range(width)] + [second + s for s in range(width)]


def amplitude_kernel(screen_ref, x_ref, out_ref, pick_ref, rows_ref):
    third = pl.program_id(0)

    @pl.when(third == 0)
    def _():
        row = lax.broadcasted_iota(jnp.int32, (HALF * VB, LANES), 0)
        col = lax.broadcasted_iota(jnp.int32, (HALF * VB, LANES), 1)
        upper = col >= HALF
        offset = row - jnp.where(upper, col - HALF, col) * VB
        columns = kept_columns(screen_ref)
        for pair in range(KEPT // 2):
            even, odd = columns[2 * pair], columns[2 * pair + 1]
            at = slice(pair * LANES, (pair + 1) * LANES)
            pick_ref[0, :, at] = jnp.where(
                offset == jnp.where(upper, odd, even), 1.0, 0.0
            ).astype(BF16)
            pick_ref[1, :, at] = jnp.where(
                offset == jnp.where(upper, even, odd), 1.0, 0.0
            ).astype(BF16)
        for o in range(ON):
            out_ref[o * YN + YN - 1, :, (UNITS - 1) * LANES:] = jnp.zeros((KSRC, LANES), BF16)

    low, high = (
        jnp.dot(
            x_ref[:, half * HALF * VB:(half + 1) * HALF * VB],
            pick_ref[half],
            preferred_element_type=F32,
        )
        for half in range(2)
    )
    lower = lax.broadcasted_iota(jnp.int32, (BO * NI, LANES), 1) < HALF
    for pair in range(KEPT // 2):
        at = slice(pair * LANES, (pair + 1) * LANES)
        even = jnp.where(lower, low[:, at], high[:, at])
        odd = jnp.where(lower, high[:, at], low[:, at])
        rows_ref[pl.ds(2 * pair, BO * NI, stride=KEPT), :] = even
        rows_ref[pl.ds(2 * pair + 1, BO * NI, stride=KEPT), :] = pltpu.roll(odd, HALF, 1)

    for now in range(THIRDS):

        @pl.when(third == now)
        def _():
            def put(kp, carry):
                rows = pl.ds(pl.multiple_of(kp * 2 * KEPT, 2 * KEPT), 2 * KEPT)
                for i in range(NI):
                    y, place = divmod(now * IL + i % IL, UNITS)
                    low = pl.multiple_of((2 * kp * NI + i) * KEPT, KEPT)
                    high = pl.multiple_of(((2 * kp + 1) * NI + i) * KEPT, KEPT)
                    tile = jnp.concatenate(
                        [rows_ref[pl.ds(low, KEPT), :], rows_ref[pl.ds(high, KEPT), :]], axis=0
                    ).astype(BF16)
                    out_ref[(i // IL) * YN + y, rows, place * LANES:(place + 1) * LANES] = tile
                return carry

            lax.fori_loop(0, BO // 2, put, 0)


def relay_amplitudes(screen, x):
    shape = (ON * YN, KSRC, WIDE)
    return pl.pallas_call(
        amplitude_kernel,
        grid=(THIRDS,),
        in_specs=[
            pl.BlockSpec(memory_space=pltpu.SMEM),
            pl.BlockSpec((BO * NI, LANES * VB), lambda t: (0, t)),
        ],
        out_specs=pl.BlockSpec(shape, lambda t: (0, 0, 0)),
        out_shape=jax.ShapeDtypeStruct(shape, BF16),
        scratch_shapes=[
            pltpu.VMEM((2, HALF * VB, KEPT * HALF), BF16),
            pltpu.VMEM((BO * NI * KEPT + KEPT, LANES), F32),
        ],
        compiler_params=pltpu.CompilerParams(vmem_limit_bytes=64 * MIB - 256 * 1024),
        cost_estimate=pl.CostEstimate(
            flops=2 * BO * NI * THIRDS * LANES * VB * KEPT * HALF,
            bytes_accessed=14 * MIB,
            transcendentals=0,
        ),
        name="relay_amplitudes",
    )(screen, x)


def integral_kernel(screen_ref, w_ref, out_ref, sum_ref):
    col = lax.broadcasted_iota(jnp.int32, (8, KW), 1)
    y_of = jnp.zeros((8, KW), jnp.int32)
    for y in range(1, YN):
        y_of = jnp.where(col >= y * KSRC, y, y_of)
    inner = col - y_of * KSRC
    wanted = jnp.full((8, KW), -(10**6), jnp.int32)
    for s, column in enumerate(kept_columns(screen_ref)):
        wanted = jnp.where(inner == s, y_of * VB + column, wanted)
    row = lax.broadcasted_iota(jnp.int32, (2 * LANES, KW), 0)
    offset = row - wanted[0:1]
    w = w_ref[...].reshape(BO * RJ, Q * VB)
    for z in range(ZN):
        start = 0 if (z + 1) * YN * VB <= 2 * LANES else LANES
        pick = jnp.where(offset == z * YN * VB - start, 1.0, 0.0).astype(BF16)
        sum_ref[...] = jnp.dot(
            w[:, start:start + 2 * LANES], pick, preferred_element_type=F32
        )
        total = sum_ref[0:RJ, :]
        for k in range(1, BO):
            total = total + pltpu.roll(sum_ref[k * RJ:(k + 1) * RJ, :], k * KEPT, 1)
        out_ref[z * RJ:(z + 1) * RJ, :] = total.astype(BF16)


def relay_integrals(screen, w):
    return pl.pallas_call(
        integral_kernel,
        in_specs=[
            pl.BlockSpec(memory_space=pltpu.SMEM),
            pl.BlockSpec(memory_space=pltpu.VMEM),
        ],
        out_specs=pl.BlockSpec(memory_space=pltpu.VMEM),
        out_shape=jax.ShapeDtypeStruct((ZN * RJ, KW), BF16),
        scratch_shapes=[
            pltpu.VMEM((BO * RJ, KW), F32),
        ],
        compiler_params=pltpu.CompilerParams(vmem_limit_bytes=62 * MIB),
        cost_estimate=pl.CostEstimate(
            flops=2 * BO * RJ * Q * VB * ZN * KW, bytes_accessed=MIB, transcendentals=0
        ),
        name="relay_integrals",
    )(screen, w)


def contract_kernel(w_ref, a_ref, out_ref):
    left = jnp.concatenate([w_ref[o, 0] for o in range(ON)], axis=1)
    product = jnp.dot(left, a_ref[...], preferred_element_type=F32)
    out_ref[...] = product.reshape(ZN, RJ, WIDE)


def contract(w, a):
    return pl.pallas_call(
        contract_kernel,
        grid=(YN,),
        in_specs=[
            pl.BlockSpec((ON, 1, ZN * RJ, KW), lambda y: (0, y, 0, 0)),
            pl.BlockSpec((ON * KW, WIDE), lambda y: (0, 0), pipeline_mode=pl.Buffered(1)),
        ],
        out_specs=pl.BlockSpec((ZN, RJ, WIDE), lambda y: (0, y, 0)),
        out_shape=jax.ShapeDtypeStruct((ZN, YN * RJ, WIDE), F32),
        compiler_params=pltpu.CompilerParams(vmem_limit_bytes=60 * MIB),
        cost_estimate=pl.CostEstimate(
            flops=2 * YN * ZN * RJ * ON * KW * WIDE, bytes_accessed=20 * MIB, transcendentals=0
        ),
        name="contract",
    )(w, a)


def store_kernel(d_ref, out_ref):
    row = lax.broadcasted_iota(jnp.int32, (LANES, LANES * VB), 0)
    col = lax.broadcasted_iota(jnp.int32, (LANES, LANES * VB), 1)
    spread = jnp.where(col // VB == row, 1.0, 0.0).astype(BF16)
    place = lax.broadcasted_iota(jnp.int32, (RJ, LANES * VB), 0) // NJ
    minor = lax.broadcasted_iota(jnp.int32, (RJ, LANES * VB), 1) % VB
    own = place == minor
    for third in range(THIRDS):
        places = [divmod(third * IL + il, UNITS) for il in range(IL)]
        pieces = [d_ref[y, :, slot * LANES:(slot + 1) * LANES] for y, slot in places]
        wide = jnp.dot(
            jnp.concatenate(pieces, axis=0), spread, preferred_element_type=F32
        )
        for il in range(IL):
            mine = jnp.where(own, wide[il * RJ:(il + 1) * RJ], 0.0)
            both = mine[0:8]
            for g in range(1, RJ // 8):
                both = both + mine[8 * g:8 * g + 8]
            out_ref[il, :, third * LANES * VB:(third + 1) * LANES * VB] = (
                both[0:NJ] + both[NJ:2 * NJ]
            ).astype(BF16)


def store(d):
    return pl.pallas_call(
        store_kernel,
        in_specs=[pl.BlockSpec(memory_space=pltpu.VMEM)],
        out_specs=pl.BlockSpec(memory_space=pltpu.VMEM),
        out_shape=jax.ShapeDtypeStruct((IL, NJ, Q * VB * VB), BF16),
        compiler_params=pltpu.CompilerParams(vmem_limit_bytes=16 * MIB),
        cost_estimate=pl.CostEstimate(
            flops=2 * IL * THIRDS * RJ * LANES * LANES * VB,
            bytes_accessed=MIB,
            transcendentals=0,
        ),
        name="store",
    )(d)


def local(t2_tiles, w_cycle, screen):
    tiles = screen.T
    x = jnp.transpose(t2_tiles, (1, 2, 0, 3)).reshape(BO * NI, Q * VB * VB)
    w = jnp.transpose(w_cycle, (0, 2, 1, 3)).reshape(BO * VB, NJ, Q * VB)
    w_part = relay_integrals(tiles, w).reshape(ZN, RJ, KW)
    w_part = lax.all_to_all(w_part, "z", 0, 0, tiled=True)
    w_part, send = lax.optimization_barrier((w_part, relay_amplitudes(tiles, x)))
    w_all = lax.all_gather(w_part, ("occ", "y"), axis=0, tiled=False)
    w_all = w_all.reshape(ON, YN, ZN * RJ, KW)
    a = lax.all_to_all(send, ("occ", "y"), 0, 0, tiled=True).reshape(ON * KW, WIDE)
    part = contract(w_all, a)
    mine = lax.psum_scatter(part, "z", scatter_dimension=0, tiled=True)
    d = mine.reshape(YN, RJ, WIDE).astype(BF16)
    d = lax.all_to_all(d, "y", 0, 0, tiled=True)
    return store(d).reshape(IL, NJ, 1, Q * VB * VB)


def solution(mesh):
    fine = Mesh(mesh.devices.reshape(ON, ZN, YN), ("occ", "z", "y"))
    vir = ("z", "y")
    placed = (P(None, "occ", vir, None), P("occ", None, vir, None), P())
    return jax.shard_map(
        local, mesh=fine, in_specs=placed, out_specs=P("occ", None, vir, None), check_vma=False
    )
```
